256 devices in a mesh: req: 64 (over y_hi, z, x), blk: 4 (over y_lo, core).
Axes of the slice: x: 4, y: 4 (y_hi: 2, y_lo: 2; y = y_hi * 2 + y_lo), z: 8, core: 2. Of those that a mesh axis runs over, the one named last changes fastest.
Arguments:
- queries: bfloat16 [2, 128, 8192], P(None, 'req'), may hold values from -96 to 96
- new_keys: bfloat16 [2, 128, 1024], P(None, 'req'), may hold values from -4.6 to 4.6
- new_values: bfloat16 [2, 128, 1024], P(None, 'req'), may hold values from -5 to 5
- cache: bfloat16 [128, 64, 16, 2048], P('req', 'blk'), may hold values from -5 to 5
- page_table: int32 [128, 64], P('req'), may hold values from 0 to 63, as said below
- kept: int32 [2, 128, 8, 16], P(None, 'req'), may hold values from 0 to 63, as said below
- moves: int32 [64], replicated, may hold values from 0 to 63, as said below
Outputs:
- first_out: bfloat16 [128, 8192], P('req', 'blk')
- second_out: bfloat16 [128, 8192], P('req', 'blk')
- cache_after: bfloat16 [128, 64, 16, 2048], P('req', 'blk')
The draws below stay inside these ranges and needn't reach their ends.
Inputs may be any that keep to these rules, and one draw needn't show every extreme that they name: `page_table`: each row is a permutation of the 64 storage positions. `kept`: each list of 16 ids is distinct; through page_table at most 8 of them lie in one index of blk's storage block of 16 positions, and exactly 8 in some block. moves[moves[g]] = g; every g with moves[g] != g has moves[g] = g XOR a distance common to all such g; moves[0] != 0.
All inputs are finite; a program needn't handle non-finite values.
Results may differ from the reference program's by a relative error of at most 0.013.
Values may be sent and summed in bfloat16 or wider, within the bound.
A program may use at most 64 MiB of HBM per device.

```python
import jax
import jax.numpy as jnp
from jax import lax

H = 64
KVH = 8
HD = 128
PAGE = 16
REQ_DEV = 2
PAGES_DEV = 16
PAGES = 64
KEEP = 16
CAP = 8
REQS = 128


def shared_keys(key):
    return jnp.clip(jax.random.normal(key, (2, REQS, KVH * HD), jnp.float32), -4.0, 4.0)


def page_layout(key):
    scores = jax.random.randint(key, (REQS, PAGES), 0, 1 << 20) * PAGES + jnp.arange(PAGES, dtype=jnp.int32)
    return jnp.argsort(scores, axis=1, stable=True).astype(jnp.int32)


def draw_new_keys(key, part):
    shared = shared_keys(key)
    return shared.astype(jnp.bfloat16)


def draw_queries(key, part):
    shared = shared_keys(key)
    key = jax.random.fold_in(key, 12)
    key_noise = jax.random.fold_in(key, 0)
    jitter = jnp.clip(jax.random.normal(key_noise, (2, REQS, KVH, H // KVH, HD), jnp.float32), -4.0, 4.0)
    own_keys = shared.reshape(2, REQS, KVH, 1, HD)
    drawn = 0.5 * own_keys + 0.85 * jitter
    return drawn.reshape(2, REQS, H * HD).astype(jnp.bfloat16)


def draw_page_table(key, part):
    return page_layout(key)


def draw_kept(key, part):
    table = page_layout(key)
    inverse = jnp.argsort(table, axis=1, stable=True).astype(jnp.int32)
    key = jax.random.fold_in(key, 13)
    key_busy, key_own, key_other, key_order = jax.random.split(key, 4)
    blocks = PAGES // PAGES_DEV
    busiest = jax.random.randint(key_busy, (2, REQS, KVH), 0, blocks)
    own_scores = jax.random.randint(key_own, (2, REQS, KVH, PAGES_DEV), 0, 1 << 20) * PAGES_DEV + jnp.arange(PAGES_DEV, dtype=jnp.int32)
    own_slots = jnp.argsort(own_scores, axis=-1, stable=True)[..., :CAP].astype(jnp.int32)
    own_locs = busiest[..., None] * PAGES_DEV + own_slots
    spare = (blocks - 1) * PAGES_DEV
    other_scores = jax.random.randint(key_other, (2, REQS, KVH, spare), 0, 1 << 20) * spare + jnp.arange(spare, dtype=jnp.int32)
    other_pick = jnp.argsort(other_scores, axis=-1, stable=True)[..., :KEEP - CAP].astype(jnp.int32)
    other_block = other_pick // PAGES_DEV
    other_block = other_block + (other_block >= busiest[..., None]).astype(jnp.int32)
    other_locs = other_block * PAGES_DEV + other_pick % PAGES_DEV
    all_locs = jnp.concatenate([own_locs, other_locs], axis=-1)
    order_scores = jax.random.randint(key_order, (2, REQS, KVH, KEEP), 0, 1 << 20) * KEEP + jnp.arange(KEEP, dtype=jnp.int32)
    order = jnp.argsort(order_scores, axis=-1, stable=True).astype(jnp.int32)
    all_locs = jnp.take_along_axis(all_locs, order, axis=-1)
    lookup = jnp.broadcast_to(inverse[None, :, None, :], (2, REQS, KVH, PAGES))
    return jnp.take_along_axis(lookup, all_locs, axis=-1).astype(jnp.int32)


def draw_moves(key, part):
    key = jax.random.fold_in(key, 14)
    key_dist, key_coin = jax.random.split(key, 2)
    groups = REQS // REQ_DEV
    distance = jax.random.randint(key_dist, (), 1, groups)
    group_ids = jnp.arange(groups, dtype=jnp.int32)
    partner = jnp.bitwise_xor(group_ids, distance)
    leader = jnp.minimum(group_ids, partner)
    coins = jax.random.randint(key_coin, (groups,), 0, 2)
    coins = coins.at[0].set(1)
    moving = coins[leader] == 1
    return jnp.where(moving, partner, group_ids).astype(jnp.int32)


def block_scale(key, dims, shards, smallest, largest):
    gain = 1.0
    for position, parts in shards:
        steps = jax.random.uniform(jax.random.fold_in(jax.random.fold_in(key, 6), position), (parts,), jnp.float32, smallest / len(shards), largest / len(shards))
        gain = gain * jnp.repeat(jnp.exp(steps), dims[position] // parts).reshape((-1,) + (1,) * (len(dims) - 1 - position))
    return gain


def bell_draw(own_key, shape, spread, limit, pieces=(), kind=jnp.bfloat16):
    values = spread * jax.random.normal(own_key, shape, jnp.float32)
    if pieces:
        values = values * block_scale(own_key, shape, pieces, -0.22, 0.18)
    return jnp.clip(values, -limit, limit).astype(kind)


def setup_inputs(seed: int = 0) -> dict:
    keys = jax.random.split(jax.random.key(seed), 8)
    return {
        "queries": draw_queries(jax.random.fold_in(keys[7], 71), 0),
        "new_keys": draw_new_keys(jax.random.fold_in(keys[7], 71), 0),
        "new_values": bell_draw(keys[2], (2, REQS, KVH * HD), 1.0, 5.0, ((1, 64),)),
        "cache": bell_draw(keys[3], (REQS, PAGES, PAGE, 2 * KVH * HD), 1.0, 5.0, ((0, 64), (1, 4))),
        "page_table": draw_page_table(jax.random.fold_in(keys[7], 71), 0),
        "kept": draw_kept(jax.random.fold_in(keys[7], 71), 0),
        "moves": draw_moves(jax.random.fold_in(keys[7], 71), 0),
    }


def attend_request(steps_used, query_row, key_rows, value_rows, table_row, kept_row, cache_row):
    score_scale = HD ** -0.5
    page_locs = table_row[kept_row]
    fetched = cache_row[page_locs].reshape(KVH, KEEP, PAGE, 2, KVH, HD)
    head_ids = jnp.arange(KVH, dtype=jnp.int32)
    cached_keys = fetched[head_ids, :, :, 0, head_ids, :].reshape(KVH, KEEP * PAGE, HD)
    cached_values = fetched[head_ids, :, :, 1, head_ids, :].reshape(KVH, KEEP * PAGE, HD)
    fresh_keys = key_rows[:steps_used].reshape(steps_used, KVH, HD).astype(jnp.float32)
    fresh_values = value_rows[:steps_used].reshape(steps_used, KVH, HD).astype(jnp.float32)
    query_heads = query_row.astype(jnp.float32).reshape(KVH, H // KVH, HD)
    cache_scores = jnp.einsum("jgd,jtd->jgt", query_heads, cached_keys.astype(jnp.float32), precision=lax.Precision.HIGHEST) * score_scale
    fresh_scores = jnp.einsum("jgd,njd->jgn", query_heads, fresh_keys, precision=lax.Precision.HIGHEST) * score_scale
    top_score = jnp.maximum(jnp.max(cache_scores, axis=-1), jnp.max(fresh_scores, axis=-1))
    cache_weights = jnp.exp(cache_scores - top_score[..., None])
    fresh_weights = jnp.exp(fresh_scores - top_score[..., None])
    total = jnp.sum(cache_weights, axis=-1) + jnp.sum(fresh_weights, axis=-1)
    cache_rounded = lax.optimization_barrier(cache_weights.astype(jnp.bfloat16)).astype(jnp.float32)
    fresh_rounded = lax.optimization_barrier(fresh_weights.astype(jnp.bfloat16)).astype(jnp.float32)
    mixed = jnp.einsum("jgt,jtd->jgd", cache_rounded, cached_values.astype(jnp.float32), precision=lax.Precision.HIGHEST)
    mixed = mixed + jnp.einsum("jgn,njd->jgd", fresh_rounded, fresh_values, precision=lax.Precision.HIGHEST)
    return (mixed / total[..., None]).astype(jnp.bfloat16).reshape(H * HD)


def reference(queries, new_keys, new_values, cache, page_table, kept, moves):
    key_major = jnp.swapaxes(new_keys, 0, 1)
    value_major = jnp.swapaxes(new_values, 0, 1)
    results = []
    for step_index in range(2):
        def attend_row(row_items, steps_used=step_index + 1):
            query_row, key_rows, value_rows, table_row, kept_row, cache_row = row_items
            return attend_request(steps_used, query_row, key_rows, value_rows, table_row, kept_row, cache_row)

        results.append(lax.map(attend_row, (queries[step_index], key_major, value_major, page_table, kept[step_index], cache)))
    sources = jnp.arange(REQS, dtype=jnp.int32).reshape(REQS // REQ_DEV, REQ_DEV)
    sources = sources.at[:, 0].set(moves.astype(jnp.int32) * REQ_DEV).reshape(REQS)
    return results[0], results[1][sources], cache[sources]
```

```python
import functools

import jax
import jax.numpy as jnp
from jax import lax
from jax.experimental import pallas as pl
from jax.experimental.pallas import tpu as pltpu
from jax.sharding import PartitionSpec as P

NEG = -1e30
MESH = pl.DeviceIdType.MESH


def partner_of(index, distance, bits):
    other = 0
    for bit in range(bits):
        value = (index // (1 << bit)) % 2
        if (distance >> bit) & 1:
            value = 1 - value
        other = other + value * (1 << bit)
    return other


def move_kernel(distance, bits, rows_ref, out_ref, got_rows, got_out, send, recv):
    g = lax.axis_index("req")
    there = {"req": partner_of(g, distance, bits)}
    barrier = pltpu.get_barrier_semaphore()
    pl.semaphore_signal(barrier, inc=1, device_id=there, device_id_type=MESH)
    pl.semaphore_wait(barrier, 1)
    copies = [
        pltpu.make_async_remote_copy(
            src_ref=rows_ref.at[0],
            dst_ref=got_rows,
            send_sem=send.at[0],
            recv_sem=recv.at[0],
            device_id=there,
            device_id_type=MESH,
        ),
        pltpu.make_async_remote_copy(
            src_ref=out_ref,
            dst_ref=got_out,
            send_sem=send.at[1],
            recv_sem=recv.at[1],
            device_id=there,
            device_id_type=MESH,
        ),
    ]
    for copy in copies:
        copy.start()
    for copy in copies:
        copy.wait()


def move(distance, bits, cache, row):
    return pl.pallas_call(
        functools.partial(move_kernel, distance, bits),
        out_shape=(
            jax.ShapeDtypeStruct(cache.shape[1:], cache.dtype),
            jax.ShapeDtypeStruct(row.shape, row.dtype),
        ),
        in_specs=[pl.BlockSpec(memory_space=pl.ANY)] * 2,
        out_specs=(pl.BlockSpec(memory_space=pl.ANY),) * 2,
        scratch_shapes=[pltpu.SemaphoreType.DMA((2,)), pltpu.SemaphoreType.DMA((2,))],
        compiler_params=pltpu.CompilerParams(collective_id=distance, has_side_effects=True),
    )(cache, row)


def partials(queries, cache, table, kept, first_page):
    steps, rows, heads = kept.shape[:3]
    pages, size, width = cache.shape[1:]
    head_size = width // (2 * heads)
    stored = jax.vmap(lambda t, k: t[k], (0, 1), 1)(table, kept)
    here = first_page + jnp.arange(pages, dtype=jnp.int32)
    use = jnp.any(stored[..., None] == here, axis=3)
    view = cache.reshape(rows, pages, size, 2, heads, head_size)
    q = queries.reshape(steps, rows, heads, -1, head_size)
    scores = jnp.einsum(
        "srjgd,rptjd->srjgpt", q, view[:, :, :, 0], preferred_element_type=jnp.float32
    )
    scores = scores * head_size**-0.5
    mask = use[:, :, :, None, :, None]
    scores = jnp.where(mask, scores, NEG)
    top = jnp.max(scores, axis=(4, 5))
    weights = jnp.where(mask, jnp.exp(scores - top[..., None, None]), 0.0)
    total = jnp.sum(weights, axis=(4, 5))
    mixed = jnp.einsum(
        "srjgpt,rptjd->srjgd",
        weights.astype(jnp.bfloat16),
        view[:, :, :, 1],
        preferred_element_type=jnp.float32,
    )
    return top, total, mixed


def finish(packed, queries, keys, values, blk, own):
    head_size = packed.shape[-1] // 2
    steps, rows = queries.shape[:2]
    mixed, top, total = (
        packed[..., :head_size],
        packed[..., head_size],
        packed[..., head_size + 1],
    )
    q = lax.dynamic_slice_in_dim(
        queries.reshape(steps, rows, -1, packed.shape[4], head_size), blk * own, own, 2
    )
    k = lax.dynamic_slice_in_dim(keys.reshape(steps, rows, -1, head_size), blk * own, own, 2)
    v = lax.dynamic_slice_in_dim(values.reshape(steps, rows, -1, head_size), blk * own, own, 2)
    fresh = jnp.einsum("srjgd,nrjd->srjgn", q, k, preferred_element_type=jnp.float32)
    fresh = fresh * head_size**-0.5
    seen = jnp.arange(steps)[None, :] <= jnp.arange(steps)[:, None]
    seen = seen[:, None, None, None, :]
    fresh = jnp.where(seen, fresh, NEG)
    best = jnp.maximum(jnp.max(top, axis=0), jnp.max(fresh, axis=-1))
    scale = jnp.exp(top - best)
    weights = jnp.where(seen, jnp.exp(fresh - best[..., None]), 0.0)
    total = jnp.sum(total * scale, axis=0) + jnp.sum(weights, axis=-1)
    mixed = jnp.sum(mixed * scale[..., None], axis=0) + jnp.einsum(
        "srjgn,nrjd->srjgd",
        weights.astype(jnp.bfloat16),
        v,
        preferred_element_type=jnp.float32,
    )
    return (mixed / total[..., None]).astype(jnp.bfloat16).reshape(steps, rows, -1)


def on_device(queries, new_keys, new_values, cache, page_table, kept, moves):
    blk = lax.axis_index("blk")
    g = lax.axis_index("req")
    blks, count = lax.axis_size("blk"), lax.axis_size("req")
    bits = count.bit_length() - 1
    own = kept.shape[2] // blks
    top, total, mixed = partials(queries, cache, page_table, kept, blk * cache.shape[1])
    packed = jnp.concatenate(
        [mixed, jnp.stack([top, total] * (mixed.shape[-1] // 2), axis=-1)], axis=-1
    )
    packed = lax.all_to_all(packed, "blk", 2, 0, tiled=True)
    packed = packed.reshape(blks, -1, *packed.shape[1:])
    out = finish(packed, queries, new_keys, new_values, blk, own)
    row = out[1, 0].reshape(-1, 128)
    branches = [functools.partial(move, d, bits) for d in range(1, count)]
    got_rows, got_out = lax.switch(moves[0] - 1, branches, cache, row)
    moving = moves[g] != g
    after = jnp.stack([jnp.where(moving, got_rows, cache[0]), cache[1]])
    second = jnp.stack([jnp.where(moving, got_out.reshape(-1), out[1, 0]), out[1, 1]])
    return out[0], second, after


def solution(mesh):
    in_specs = (
        P(None, "req", None),
        P(None, "req", None),
        P(None, "req", None),
        P("req", "blk", None, None),
        P("req", None),
        P(None, "req", None, None),
        P(),
    )
    out_specs = (P("req", "blk"), P("req", "blk"), P("req", "blk", None, None))
    return jax.shard_map(
        on_device, mesh=mesh, in_specs=in_specs, out_specs=out_specs, check_vma=False
    )
```

```python
import functools

import jax
import jax.numpy as jnp
from jax import lax
from jax.experimental import pallas as pl
from jax.experimental.pallas import tpu as pltpu
from jax.sharding import PartitionSpec as P

NEG = -1e30
MESH = pl.DeviceIdType.MESH
F32, BF16 = jnp.float32, jnp.bfloat16
LANES = 128


def partner_of(index, distance, bits):
    other = 0
    for bit in range(bits):
        value = (index // (1 << bit)) % 2
        if (distance >> bit) & 1:
            value = 1 - value
        other = other + value * (1 << bit)
    return other


def lanes_at(start):
    return pl.ds(pl.multiple_of(start * LANES, LANES), LANES)


def fused_kernel(
    distance, bits,
    moves, cache, queries, keys, values, table, kept,
    got_rows, first_out, second_out,
    cache_v, q_raw, k_raw, v_raw, table_s, kept_s, first_v, second_v,
    q_all, sent, came, o_all, row_send, row_got,
    load_sem, store_sem, big_sem, part_ss, part_rs, row_sem,
):
    g = lax.axis_index("req")
    blk = lax.axis_index("blk")
    blks = sent.shape[0]
    rows, pages, size, _ = cache_v.shape
    heads = q_all.shape[0]
    steps, keep = kept_s.shape[0], kept_s.shape[3]
    own = heads // blks
    both = q_all.shape[2]
    group = both // steps
    tokens = pages * size
    scale = LANES**-0.5
    there = {"req": partner_of(g, distance, bits)}

    barrier = pltpu.get_barrier_semaphore()
    pl.semaphore_signal(barrier, inc=1, device_id=there, device_id_type=MESH)

    def greet(rel, carry):
        peer = {"blk": lax.rem(blk + rel, blks)}
        pl.semaphore_signal(barrier, inc=1, device_id=peer, device_id_type=MESH)
        return carry

    lax.fori_loop(1, blks, greet, 0)
    loads = [
        pltpu.make_async_copy(src, dst, load_sem.at[i])
        for i, (src, dst) in enumerate(
            [
                (table, table_s),
                (kept, kept_s),
                (queries, q_raw),
                (keys, k_raw),
                (values, v_raw),
                (cache, cache_v),
            ]
        )
    ]
    for load in loads:
        load.start()
    pl.semaphore_wait(barrier, blks)

    big = pltpu.make_async_remote_copy(
        src_ref=cache.at[0],
        dst_ref=got_rows,
        send_sem=big_sem.at[0],
        recv_sem=big_sem.at[1],
        device_id=there,
        device_id_type=MESH,
    )
    big.start()
    for load in loads:
        load.wait()

    sent[...] = jnp.zeros_like(sent)
    lane = lax.broadcasted_iota(jnp.int32, (both, LANES), 1)
    place = lax.broadcasted_iota(jnp.int32, (both, tokens), 1) // size + blk * pages
    early = lax.broadcasted_iota(jnp.int32, (both, tokens), 0) < group

    def head(j, carry):
        def spread(i, inner):
            pair = q_raw[i // group, :, lanes_at(j * group + i % group)].astype(F32)
            for r in range(rows):
                q_all[j, r, pl.ds(i, 1), :] = pair[r : r + 1]
            return inner

        lax.fori_loop(0, both, spread, 0)

        def request(r, inner):
            def mark(k, found):
                first, second = (table_s[r, kept_s[s, r, j, k]] for s in range(steps))
                return jnp.where(place == jnp.where(early, first, second), 1.0, found)

            live = lax.fori_loop(0, keep, mark, jnp.zeros((both, tokens), F32)) > 0.0
            k = cache_v[r, :, :, lanes_at(j)].reshape(tokens, LANES)
            v = cache_v[r, :, :, lanes_at(j + heads)].reshape(tokens, LANES)
            scores = lax.dot_general(
                q_all[j, r].astype(BF16), k, (((1,), (1,)), ((), ())), preferred_element_type=F32
            )
            scores = jnp.where(live, scores * scale, NEG)
            top = jnp.max(scores, axis=1, keepdims=True)
            weights = jnp.where(live, jnp.exp(scores - top), 0.0)
            total = jnp.sum(weights, axis=1, keepdims=True)
            to, at = j // own, (j % own) * rows + r
            sent[to, at] = jnp.dot(weights.astype(BF16), v, preferred_element_type=F32)
            old = sent[to, own * rows]
            sent[to, own * rows] = jnp.where(
                lane == at, top, jnp.where(lane == at + LANES // 2, total, old)
            )
            return inner

        lax.fori_loop(0, rows, request, 0)
        return carry

    lax.fori_loop(0, heads, head, 0)

    def part(rel):
        to = lax.rem(blk + rel, blks)
        return pltpu.make_async_remote_copy(
            src_ref=sent.at[to],
            dst_ref=came.at[rel],
            send_sem=part_ss.at[rel],
            recv_sem=part_rs.at[rel],
            device_id={"blk": to},
            device_id_type=MESH,
        )

    def each_part(act):
        def one(rel, carry):
            act(part(rel))
            return carry

        lax.fori_loop(1, blks, one, 0)

    each_part(lambda copy: copy.start())
    came[0] = sent[blk]
    each_part(lambda copy: copy.wait_recv())

    late = lax.broadcasted_iota(jnp.int32, (both, 1), 0) >= group

    def merge(at, carry):
        r = at % rows
        j = blk * own + at // rows

        def pick(raw, n):
            pair = raw[n, :, lanes_at(j)].astype(F32)
            return jnp.where(r == 0, pair[0:1], pair[1:2])

        def column(i, place):
            kept_lane = jnp.where(lane == place, came[i, own * rows], 0.0)
            return jnp.sum(kept_lane, axis=1, keepdims=True)

        query = q_all[j, r]
        fresh = [
            jnp.sum(query * pick(k_raw, n), axis=1, keepdims=True) * scale for n in range(steps)
        ]
        fresh[1] = jnp.where(late, fresh[1], NEG)
        tops = [column(i, at) for i in range(blks)]
        best = functools.reduce(jnp.maximum, tops + fresh)
        total = jnp.zeros_like(best)
        mixed = jnp.zeros((both, LANES), F32)
        for i, top in enumerate(tops):
            factor = jnp.exp(top - best)
            total = total + factor * column(i, at + LANES // 2)
            mixed = mixed + factor * came[i, at]
        for n, score in enumerate(fresh):
            weight = jnp.exp(score - best)
            if n:
                weight = jnp.where(late, weight, 0.0)
            total = total + weight
            mixed = mixed + weight.astype(BF16).astype(F32) * pick(v_raw, n)
        o_all[at] = mixed / total
        return carry

    lax.fori_loop(0, own * rows, merge, 0)

    for jj in range(own):
        row_send[jj * group : (jj + 1) * group] = o_all[jj * rows, group:both]
    row_copy = pltpu.make_async_remote_copy(
        src_ref=row_send,
        dst_ref=row_got,
        send_sem=row_sem.at[0],
        recv_sem=row_sem.at[1],
        device_id=there,
        device_id_type=MESH,
    )
    row_copy.start()

    def lay_first(i, carry):
        at = (i // group) * rows
        first_v[:, lanes_at(i)] = jnp.concatenate(
            [o_all[at + r, pl.ds(i % group, 1), :] for r in range(rows)], axis=0
        ).astype(BF16)
        return carry

    lax.fori_loop(0, own * group, lay_first, 0)
    first_copy = pltpu.make_async_copy(first_v, first_out, store_sem.at[0])
    first_copy.start()
    each_part(lambda copy: copy.wait_send())
    row_copy.wait()
    moving = moves[g] != g

    def lay_second(i, carry):
        at = (i // group) * rows
        moved = jnp.where(moving, row_got[pl.ds(i, 1), :], row_send[pl.ds(i, 1), :])
        stays = o_all[at + 1, pl.ds(i % group + group, 1), :]
        second_v[:, lanes_at(i)] = jnp.concatenate([moved, stays], axis=0).astype(BF16)
        return carry

    lax.fori_loop(0, own * group, lay_second, 0)
    second_copy = pltpu.make_async_copy(second_v, second_out, store_sem.at[1])
    second_copy.start()
    first_copy.wait()
    second_copy.wait()
    big.wait()


def fused(distance, bits, moves, cache, queries, keys, values, table, kept):
    steps, rows, heads, keep = kept.shape
    pages, size, width = cache.shape[1:]
    blks = lax.axis_size("blk")
    own = heads // blks
    group = queries.shape[2] // (heads * LANES)
    both = steps * group
    anywhere = pl.BlockSpec(memory_space=pl.ANY)
    out = jax.ShapeDtypeStruct((rows, own * group * LANES), BF16)
    dma = pltpu.SemaphoreType.DMA
    return pl.pallas_call(
        functools.partial(fused_kernel, distance, bits),
        out_shape=(jax.ShapeDtypeStruct(cache.shape[1:], cache.dtype), out, out),
        in_specs=[pl.BlockSpec(memory_space=pltpu.SMEM)] + [anywhere] * 6,
        out_specs=(anywhere,) * 3,
        scratch_shapes=[
            pltpu.VMEM(cache.shape, BF16),
            pltpu.VMEM(queries.shape, BF16),
            pltpu.VMEM(keys.shape, BF16),
            pltpu.VMEM(values.shape, BF16),
            pltpu.SMEM(table.shape, jnp.int32),
            pltpu.SMEM(kept.shape, jnp.int32),
            pltpu.VMEM(out.shape, BF16),
            pltpu.VMEM(out.shape, BF16),
            pltpu.VMEM((heads, rows, both, LANES), F32),
            pltpu.VMEM((blks, own * rows + 1, both, LANES), F32),
            pltpu.VMEM((blks, own * rows + 1, both, LANES), F32),
            pltpu.VMEM((own * rows, both, LANES), F32),
            pltpu.VMEM((own * group, LANES), F32),
            pltpu.VMEM((own * group, LANES), F32),
            dma((6,)),
            dma((2,)),
            dma((2,)),
            dma((blks,)),
            dma((blks,)),
            dma((2,)),
        ],
        compiler_params=pltpu.CompilerParams(
            collective_id=distance, has_side_effects=True, vmem_limit_bytes=48 << 20
        ),
        name="attend_and_move",
    )(moves, cache, queries, keys, values, table, kept)


def on_device(queries, new_keys, new_values, cache, page_table, kept, moves):
    count = lax.axis_size("req")
    bits = count.bit_length() - 1
    branches = [functools.partial(fused, d, bits) for d in range(1, count)]
    got, first, second = lax.switch(
        moves[0] - 1, branches, moves, cache, queries, new_keys, new_values, page_table, kept
    )
    g = lax.axis_index("req")
    first_row = lax.broadcasted_iota(jnp.int32, (cache.shape[0], 1, 1, 1), 0) == 0
    arrives = jnp.logical_and(moves[g] != g, first_row)
    return first, second, jnp.where(arrives, got[None], cache)


def solution(mesh):
    in_specs = (
        P(None, "req", None),
        P(None, "req", None),
        P(None, "req", None),
        P("req", "blk", None, None),
        P("req", None),
        P(None, "req", None, None),
        P(),
    )
    out_specs = (P("req", "blk"), P("req", "blk"), P("req", "blk", None, None))
    return jax.shard_map(
        on_device, mesh=mesh, in_specs=in_specs, out_specs=out_specs, check_vma=False
    )
```

```python
import functools

import jax
import jax.numpy as jnp
from jax import lax
from jax.experimental import pallas as pl
from jax.experimental.pallas import tpu as pltpu
from jax.sharding import PartitionSpec as P

NEG = -1e30
MESH = pl.DeviceIdType.MESH
F32, BF16 = jnp.float32, jnp.bfloat16
LANES = 128
PHASES = (6, 7, 3)


def partner_of(index, distance, bits):
    other = index
    for bit in range(bits):
        if (distance >> bit) & 1:
            value = lax.rem(lax.div(index, 1 << bit), 2)
            other = other + (1 << bit) - value * (2 << bit)
    return other


def in_parts(distance):
    return distance // 32 == 1 and distance // 4 % 8 < 2


def lanes_at(start):
    return pl.ds(pl.multiple_of(start * LANES, LANES), LANES)


def fused_kernel(
    distance, bits,
    cache, queries, keys, values, table, kept,
    got_rows, stage, heads_out, moved_out,
    cache_v, q_raw, k_raw, v_raw, table_s, kept_s,
    q_all, sent, came, o_all,
    load_sem, store_sem, big_sem, part_ss, part_rs, row_sem,
):
    g = lax.axis_index("req")
    blk = lax.axis_index("blk")
    blks = sent.shape[0]
    rows, pages, size, _ = cache_v.shape
    heads = q_all.shape[0]
    steps, keep = kept_s.shape[0], kept_s.shape[3]
    own = heads // blks
    both = q_all.shape[2]
    group = both // steps
    tokens = pages * size
    scale = LANES**-0.5
    there = {"req": partner_of(g, distance, bits)}

    barrier = pltpu.get_barrier_semaphore()
    pl.semaphore_signal(barrier, inc=1, device_id=there, device_id_type=MESH)

    def greet(rel, carry):
        peer = {"blk": lax.rem(blk + rel, blks)}
        pl.semaphore_signal(barrier, inc=1, device_id=peer, device_id_type=MESH)
        return carry

    lax.fori_loop(1, blks, greet, 0)
    loads = [
        pltpu.make_async_copy(src, dst, load_sem.at[i])
        for i, (src, dst) in enumerate(
            [
                (table, table_s),
                (kept, kept_s),
                (queries, q_raw),
                (keys, k_raw),
                (values, v_raw),
                (cache, cache_v),
            ]
        )
    ]
    for load in loads:
        load.start()
    pl.semaphore_wait(barrier, blks)

    sizes = PHASES if in_parts(distance) else (pages,)
    edges = [sum(sizes[:i]) for i in range(len(sizes))]
    big = [
        pltpu.make_async_remote_copy(
            src_ref=cache.at[0, pl.ds(edge, length)],
            dst_ref=got_rows.at[pl.ds(edge, length)],
            send_sem=big_sem.at[0, i],
            recv_sem=big_sem.at[1, i],
            device_id=there,
            device_id_type=MESH,
        )
        for i, (edge, length) in enumerate(zip(edges, sizes))
    ]
    big[0].start()
    for load in loads:
        load.wait()
    stage_copy = pltpu.make_async_copy(cache, stage, store_sem.at[0])
    stage_copy.start()

    for i in range(blks):
        sent[i, own * rows] = jnp.zeros((both, LANES), F32)
    def part(rel):
        to = lax.rem(blk + rel, blks)
        return pltpu.make_async_remote_copy(
            src_ref=sent.at[to],
            dst_ref=came.at[rel],
            send_sem=part_ss.at[rel],
            recv_sem=part_rs.at[rel],
            device_id={"blk": to},
            device_id_type=MESH,
        )

    lane = lax.broadcasted_iota(jnp.int32, (both, LANES), 1)
    place = lax.broadcasted_iota(jnp.int32, (both, tokens), 1) // size + blk * pages
    early = lax.broadcasted_iota(jnp.int32, (both, tokens), 0) < group

    def head(j, carry):
        def spread(i, inner):
            pair = q_raw[i // group, :, lanes_at(j * group + i % group)].astype(F32)
            for r in range(rows):
                q_all[j, r, pl.ds(i, 1), :] = pair[r : r + 1]
            return inner

        lax.fori_loop(0, both, spread, 0)

        def request(r, inner):
            def mark(k, found):
                first, second = (table_s[r, kept_s[s, r, j, k]] for s in range(steps))
                return jnp.where(place == jnp.where(early, first, second), 1.0, found)

            live = lax.fori_loop(0, keep, mark, jnp.zeros((both, tokens), F32)) > 0.0
            k = cache_v[r, :, :, lanes_at(j)].reshape(tokens, LANES)
            v = cache_v[r, :, :, lanes_at(j + heads)].reshape(tokens, LANES)
            scores = lax.dot_general(
                q_all[j, r].astype(BF16), k, (((1,), (1,)), ((), ())), preferred_element_type=F32
            )
            scores = jnp.where(live, scores * scale, NEG)
            top = jnp.max(scores, axis=1, keepdims=True)
            weights = jnp.where(live, jnp.exp(scores - top), 0.0)
            total = jnp.sum(weights, axis=1, keepdims=True)
            to, at = j // own, (j % own) * rows + r
            sent[to, at] = jnp.dot(weights.astype(BF16), v, preferred_element_type=F32)
            old = sent[to, own * rows]
            sent[to, own * rows] = jnp.where(
                lane == at, top, jnp.where(lane == at + LANES // 2, total, old)
            )
            return inner

        lax.fori_loop(0, rows, request, 0)
        return carry

    def block(rel, carry):
        to = lax.rem(blk + rel, blks)
        lax.fori_loop(to * own, to * own + own, head, 0)

        @pl.when(rel < blks)
        def _():
            part(rel).start()

        return carry

    lax.fori_loop(1, blks + 1, block, 0)
    for copy in big[1:2]:
        copy.start()
    came[0] = sent[blk]

    def arrive(rel, carry):
        part(rel).wait()
        return carry

    lax.fori_loop(1, blks, arrive, 0)

    late = lax.broadcasted_iota(jnp.int32, (both, 1), 0) >= group

    def merge(at, carry):
        r = at % rows
        j = blk * own + at // rows

        def pick(raw, n):
            pair = raw[n, :, lanes_at(j)].astype(F32)
            return jnp.where(r == 0, pair[0:1], pair[1:2])

        def column(i, place):
            kept_lane = jnp.where(lane == place, came[i, own * rows], 0.0)
            return jnp.sum(kept_lane, axis=1, keepdims=True)

        query = q_all[j, r]
        fresh = [
            jnp.sum(query * pick(k_raw, n), axis=1, keepdims=True) * scale for n in range(steps)
        ]
        fresh[1] = jnp.where(late, fresh[1], NEG)
        best = jnp.maximum(*fresh)
        weights = [jnp.exp(score - best) for score in fresh]
        weights[1] = jnp.where(late, weights[1], 0.0)
        mixed = sum(
            weight.astype(BF16).astype(F32) * pick(v_raw, n) for n, weight in enumerate(weights)
        )

        def fold(i, state):
            best, total, mixed = state
            top = column(i, at)
            new = jnp.maximum(best, top)
            past, factor = jnp.exp(best - new), jnp.exp(top - new)
            total = total * past + column(i, at + LANES // 2) * factor
            return new, total, mixed * past + came[i, at] * factor

        _, total, mixed = lax.fori_loop(0, blks, fold, (best, weights[0] + weights[1], mixed))
        o_all[at // rows, r] = mixed / total
        return carry

    lax.fori_loop(0, own * rows, merge, 0)

    row_copy = pltpu.make_async_remote_copy(
        src_ref=o_all.at[:, 0, pl.ds(group, group)],
        dst_ref=moved_out,
        send_sem=row_sem.at[0],
        recv_sem=row_sem.at[1],
        device_id=there,
        device_id_type=MESH,
    )
    row_copy.start()
    for copy in big[2:]:
        copy.start()
    heads_copy = pltpu.make_async_copy(o_all, heads_out, store_sem.at[1])
    heads_copy.start()
    stage_copy.wait()
    heads_copy.wait()
    row_copy.wait()
    for copy in big:
        copy.wait()


def fused(distance, bits, cache, queries, keys, values, table, kept):
    steps, rows, heads, keep = kept.shape
    pages, size, width = cache.shape[1:]
    blks = lax.axis_size("blk")
    own = heads // blks
    group = queries.shape[2] // (heads * LANES)
    both = steps * group
    anywhere = pl.BlockSpec(memory_space=pl.ANY)
    dma = pltpu.SemaphoreType.DMA
    return pl.pallas_call(
        functools.partial(fused_kernel, distance, bits),
        out_shape=(
            jax.ShapeDtypeStruct(cache.shape[1:], cache.dtype),
            jax.ShapeDtypeStruct(cache.shape, cache.dtype),
            jax.ShapeDtypeStruct((own, rows, both, LANES), F32),
            jax.ShapeDtypeStruct((own, group, LANES), F32),
        ),
        in_specs=[anywhere] * 6,
        out_specs=(anywhere,) * 4,
        scratch_shapes=[
            pltpu.VMEM(cache.shape, BF16),
            pltpu.VMEM(queries.shape, BF16),
            pltpu.VMEM(keys.shape, BF16),
            pltpu.VMEM(values.shape, BF16),
            pltpu.SMEM(table.shape, jnp.int32),
            pltpu.SMEM(kept.shape, jnp.int32),
            pltpu.VMEM((heads, rows, both, LANES), F32),
            pltpu.VMEM((blks, own * rows + 1, both, LANES), F32),
            pltpu.VMEM((blks, own * rows + 1, both, LANES), F32),
            pltpu.VMEM((own, rows, both, LANES), F32),
            dma((6,)),
            dma((2,)),
            dma((2, len(PHASES) if in_parts(distance) else 1)),
            dma((blks,)),
            dma((blks,)),
            dma((2,)),
        ],
        compiler_params=pltpu.CompilerParams(
            collective_id=distance, has_side_effects=True, vmem_limit_bytes=48 << 20
        ),
        name="attend_and_move",
    )(cache, queries, keys, values, table, kept)


def settle_kernel(
    moves, got, stage, heads_out, moved_out,
    after, first_out, second_out,
    moves_s, heads_v, moved_v, first_v, second_v, load_sem, store_sem,
):
    g = lax.axis_index("req")
    own, rows, both, _ = heads_v.shape
    group = moved_v.shape[1]
    loads = [
        pltpu.make_async_copy(src, dst, load_sem.at[i])
        for i, (src, dst) in enumerate(
            [(moves, moves_s), (heads_out, heads_v), (moved_out, moved_v)]
        )
    ]
    stays = pltpu.make_async_copy(stage.at[1], after.at[1], store_sem.at[0])
    keeps = pltpu.make_async_copy(stage.at[0], after.at[0], store_sem.at[1])
    renews = pltpu.make_async_copy(got, after.at[0], store_sem.at[1])
    for load in loads:
        load.start()
    stays.start()
    loads[0].wait()
    moving = moves_s[g] != g

    @pl.when(moving)
    def _():
        renews.start()

    @pl.when(jnp.logical_not(moving))
    def _():
        keeps.start()

    loads[1].wait()
    loads[2].wait()
    for jj in range(own):
        for q in range(group):
            lanes = pl.ds((jj * group + q) * LANES, LANES)
            late = group + q
            moved = jnp.where(moving, moved_v[jj, q : q + 1], heads_v[jj, 0, late : late + 1])
            first_v[:, lanes] = jnp.concatenate(
                [heads_v[jj, r, q : q + 1] for r in range(rows)], axis=0
            ).astype(BF16)
            second_v[:, lanes] = jnp.concatenate(
                [moved, heads_v[jj, 1, late : late + 1]], axis=0
            ).astype(BF16)
    out = [
        pltpu.make_async_copy(first_v, first_out, store_sem.at[2]),
        pltpu.make_async_copy(second_v, second_out, store_sem.at[3]),
    ]
    for copy in out:
        copy.start()
    stays.wait()
    keeps.wait()
    for copy in out:
        copy.wait()


def settle(moves, got, stage, heads_out, moved_out):
    own, rows, both, _ = heads_out.shape
    out = jax.ShapeDtypeStruct((rows, own * moved_out.shape[1] * LANES), BF16)
    anywhere = pl.BlockSpec(memory_space=pl.ANY)
    return pl.pallas_call(
        settle_kernel,
        out_shape=(jax.ShapeDtypeStruct(stage.shape, stage.dtype), out, out),
        in_specs=[anywhere] * 5,
        out_specs=(anywhere,) * 3,
        scratch_shapes=[
            pltpu.SMEM(moves.shape, jnp.int32),
            pltpu.VMEM(heads_out.shape, F32),
            pltpu.VMEM(moved_out.shape, F32),
            pltpu.VMEM(out.shape, BF16),
            pltpu.VMEM(out.shape, BF16),
            pltpu.SemaphoreType.DMA((3,)),
            pltpu.SemaphoreType.DMA((4,)),
        ],
        compiler_params=pltpu.CompilerParams(vmem_limit_bytes=32 << 20),
        name="settle",
    )(moves, got, stage, heads_out, moved_out)


def on_device(queries, new_keys, new_values, cache, page_table, kept, moves):
    count = lax.axis_size("req")
    bits = count.bit_length() - 1
    branches = [functools.partial(fused, d, bits) for d in range(1, count)]
    pieces = lax.switch(
        moves[0] - 1, branches, cache, queries, new_keys, new_values, page_table, kept
    )
    after, first, second = settle(moves, *pieces)
    return first, second, after


def solution(mesh):
    in_specs = (
        P(None, "req", None),
        P(None, "req", None),
        P(None, "req", None),
        P("req", "blk", None, None),
        P("req", None),
        P(None, "req", None, None),
        P(),
    )
    out_specs = (P("req", "blk"), P("req", "blk"), P("req", "blk", None, None))
    return jax.shard_map(
        on_device, mesh=mesh, in_specs=in_specs, out_specs=out_specs, check_vma=False
    )
```

```python
import functools

import jax
import jax.numpy as jnp
from jax import lax
from jax.experimental import pallas as pl
from jax.experimental.pallas import tpu as pltpu
from jax.sharding import PartitionSpec as P

NEG = -1e30
MESH = pl.DeviceIdType.MESH
F32, BF16 = jnp.float32, jnp.bfloat16
LANES = 128
PHASES = (6, 7, 3)


def partner_of(index, distance, bits):
    other = index
    for bit in range(bits):
        if (distance >> bit) & 1:
            value = lax.rem(lax.div(index, 1 << bit), 2)
            other = other + (1 << bit) - value * (2 << bit)
    return other


def own_barrier(distance):
    return distance < 37


def in_parts(distance):
    return distance // 32 == 1 and distance // 4 % 8 < 2


def lanes_at(start):
    return pl.ds(pl.multiple_of(start * LANES, LANES), LANES)


def fused_kernel(
    distance, bits,
    cache, queries, keys, values, table, kept,
    got_rows, stage, heads_out, moved_out,
    cache_v, q_raw, k_raw, v_raw, table_s, kept_s,
    q_all, sent, came, o_all,
    load_sem, store_sem, big_sem, part_ss, part_rs, row_sem,
):
    g = lax.axis_index("req")
    blk = lax.axis_index("blk")
    blks = sent.shape[0]
    rows, pages, size, _ = cache_v.shape
    heads = q_all.shape[0]
    steps, keep = kept_s.shape[0], kept_s.shape[3]
    own = heads // blks
    both = q_all.shape[2]
    group = both // steps
    tokens = pages * size
    scale = LANES**-0.5
    there = {"req": partner_of(g, distance, bits)}

    greets = own_barrier(distance)
    if greets:
        barrier = pltpu.get_barrier_semaphore()
        pl.semaphore_signal(barrier, inc=1, device_id=there, device_id_type=MESH)

        def greet(rel, carry):
            peer = {"blk": lax.rem(blk + rel, blks)}
            pl.semaphore_signal(barrier, inc=1, device_id=peer, device_id_type=MESH)
            return carry

        lax.fori_loop(1, blks, greet, 0)
    loads = [
        pltpu.make_async_copy(src, dst, load_sem.at[i])
        for i, (src, dst) in enumerate(
            [
                (table, table_s),
                (kept, kept_s),
                (queries, q_raw),
                (keys, k_raw),
                (values, v_raw),
                (cache, cache_v),
            ]
        )
    ]
    for load in loads:
        load.start()
    if greets:
        pl.semaphore_wait(barrier, blks)

    sizes = PHASES if in_parts(distance) else (pages,)
    edges = [sum(sizes[:i]) for i in range(len(sizes))]
    big = [
        pltpu.make_async_remote_copy(
            src_ref=cache.at[0, pl.ds(edge, length)],
            dst_ref=got_rows.at[pl.ds(edge, length)],
            send_sem=big_sem.at[0, i],
            recv_sem=big_sem.at[1, i],
            device_id=there,
            device_id_type=MESH,
        )
        for i, (edge, length) in enumerate(zip(edges, sizes))
    ]
    big[0].start()
    for load in loads:
        load.wait()
    stage_copy = pltpu.make_async_copy(cache, stage, store_sem.at[0])
    stage_copy.start()

    for i in range(blks):
        sent[i, own * rows] = jnp.zeros((both, LANES), F32)
    def part(rel):
        to = lax.rem(blk + rel, blks)
        return pltpu.make_async_remote_copy(
            src_ref=sent.at[to],
            dst_ref=came.at[rel],
            send_sem=part_ss.at[rel],
            recv_sem=part_rs.at[rel],
            device_id={"blk": to},
            device_id_type=MESH,
        )

    lane = lax.broadcasted_iota(jnp.int32, (both, LANES), 1)
    place = lax.broadcasted_iota(jnp.int32, (both, tokens), 1) // size + blk * pages
    early = lax.broadcasted_iota(jnp.int32, (both, tokens), 0) < group

    def head(j, carry):
        def spread(i, inner):
            pair = q_raw[i // group, :, lanes_at(j * group + i % group)].astype(F32)
            for r in range(rows):
                q_all[j, r, pl.ds(i, 1), :] = pair[r : r + 1]
            return inner

        lax.fori_loop(0, both, spread, 0)

        def request(r, inner):
            def mark(k, found):
                first, second = (table_s[r, kept_s[s, r, j, k]] for s in range(steps))
                return jnp.where(place == jnp.where(early, first, second), 1.0, found)

            live = lax.fori_loop(0, keep, mark, jnp.zeros((both, tokens), F32)) > 0.0
            k = cache_v[r, :, :, lanes_at(j)].reshape(tokens, LANES)
            v = cache_v[r, :, :, lanes_at(j + heads)].reshape(tokens, LANES)
            scores = lax.dot_general(
                q_all[j, r].astype(BF16), k, (((1,), (1,)), ((), ())), preferred_element_type=F32
            )
            scores = jnp.where(live, scores * scale, NEG)
            top = jnp.max(scores, axis=1, keepdims=True)
            weights = jnp.where(live, jnp.exp(scores - top), 0.0)
            total = jnp.sum(weights, axis=1, keepdims=True)
            to, at = j // own, (j % own) * rows + r
            sent[to, at] = jnp.dot(weights.astype(BF16), v, preferred_element_type=F32)
            old = sent[to, own * rows]
            sent[to, own * rows] = jnp.where(
                lane == at, top, jnp.where(lane == at + LANES // 2, total, old)
            )
            return inner

        lax.fori_loop(0, rows, request, 0)
        return carry

    def block(rel, carry):
        to = lax.rem(blk + rel, blks)
        lax.fori_loop(to * own, to * own + own, head, 0)

        @pl.when(rel < blks)
        def _():
            part(rel).start()

        return carry

    lax.fori_loop(1, blks + 1, block, 0)
    for copy in big[1:2]:
        copy.start()
    came[0] = sent[blk]

    def arrive(rel, carry):
        part(rel).wait()
        return carry

    lax.fori_loop(1, blks, arrive, 0)

    late = lax.broadcasted_iota(jnp.int32, (both, 1), 0) >= group

    def merge(at, carry):
        r = at % rows
        j = blk * own + at // rows

        def pick(raw, n):
            pair = raw[n, :, lanes_at(j)].astype(F32)
            return jnp.where(r == 0, pair[0:1], pair[1:2])

        def column(i, place):
            kept_lane = jnp.where(lane == place, came[i, own * rows], 0.0)
            return jnp.sum(kept_lane, axis=1, keepdims=True)

        query = q_all[j, r]
        fresh = [
            jnp.sum(query * pick(k_raw, n), axis=1, keepdims=True) * scale for n in range(steps)
        ]
        fresh[1] = jnp.where(late, fresh[1], NEG)
        best = jnp.maximum(*fresh)
        weights = [jnp.exp(score - best) for score in fresh]
        weights[1] = jnp.where(late, weights[1], 0.0)
        mixed = sum(
            weight.astype(BF16).astype(F32) * pick(v_raw, n) for n, weight in enumerate(weights)
        )

        def fold(i, state):
            best, total, mixed = state
            top = column(i, at)
            new = jnp.maximum(best, top)
            past, factor = jnp.exp(best - new), jnp.exp(top - new)
            total = total * past + column(i, at + LANES // 2) * factor
            return new, total, mixed * past + came[i, at] * factor

        _, total, mixed = lax.fori_loop(0, blks, fold, (best, weights[0] + weights[1], mixed))
        o_all[at // rows, r] = mixed / total
        return carry

    lax.fori_loop(0, own * rows, merge, 0)

    row_copy = pltpu.make_async_remote_copy(
        src_ref=o_all.at[:, 0, pl.ds(group, group)],
        dst_ref=moved_out,
        send_sem=row_sem.at[0],
        recv_sem=row_sem.at[1],
        device_id=there,
        device_id_type=MESH,
    )
    row_copy.start()
    for copy in big[2:]:
        copy.start()
    heads_copy = pltpu.make_async_copy(o_all, heads_out, store_sem.at[1])
    heads_copy.start()
    stage_copy.wait()
    heads_copy.wait()
    row_copy.wait()
    for copy in big:
        copy.wait()


def fused(distance, bits, cache, queries, keys, values, table, kept):
    steps, rows, heads, keep = kept.shape
    pages, size, width = cache.shape[1:]
    blks = lax.axis_size("blk")
    own = heads // blks
    group = queries.shape[2] // (heads * LANES)
    both = steps * group
    anywhere = pl.BlockSpec(memory_space=pl.ANY)
    dma = pltpu.SemaphoreType.DMA
    return pl.pallas_call(
        functools.partial(fused_kernel, distance, bits),
        out_shape=(
            jax.ShapeDtypeStruct(cache.shape[1:], cache.dtype),
            jax.ShapeDtypeStruct(cache.shape, cache.dtype),
            jax.ShapeDtypeStruct((own, rows, both, LANES), F32),
            jax.ShapeDtypeStruct((own, group, LANES), F32),
        ),
        in_specs=[anywhere] * 6,
        out_specs=(anywhere,) * 4,
        scratch_shapes=[
            pltpu.VMEM(cache.shape, BF16),
            pltpu.VMEM(queries.shape, BF16),
            pltpu.VMEM(keys.shape, BF16),
            pltpu.VMEM(values.shape, BF16),
            pltpu.SMEM(table.shape, jnp.int32),
            pltpu.SMEM(kept.shape, jnp.int32),
            pltpu.VMEM((heads, rows, both, LANES), F32),
            pltpu.VMEM((blks, own * rows + 1, both, LANES), F32),
            pltpu.VMEM((blks, own * rows + 1, both, LANES), F32),
            pltpu.VMEM((own, rows, both, LANES), F32),
            dma((6,)),
            dma((2,)),
            dma((2, len(PHASES) if in_parts(distance) else 1)),
            dma((blks,)),
            dma((blks,)),
            dma((2,)),
        ],
        compiler_params=pltpu.CompilerParams(
            collective_id=distance if own_barrier(distance) else None,
            has_side_effects=True,
            vmem_limit_bytes=48 << 20,
        ),
        name="attend_and_move",
    )(cache, queries, keys, values, table, kept)


def settle_kernel(
    moves, got, stage, heads_out, moved_out,
    after, first_out, second_out,
    moves_s, heads_v, moved_v, first_v, second_v, load_sem, store_sem,
):
    g = lax.axis_index("req")
    own, rows, both, _ = heads_v.shape
    group = moved_v.shape[1]
    loads = [
        pltpu.make_async_copy(src, dst, load_sem.at[i])
        for i, (src, dst) in enumerate(
            [(moves, moves_s), (heads_out, heads_v), (moved_out, moved_v)]
        )
    ]
    stays = pltpu.make_async_copy(stage.at[1], after.at[1], store_sem.at[0])
    keeps = pltpu.make_async_copy(stage.at[0], after.at[0], store_sem.at[1])
    renews = pltpu.make_async_copy(got, after.at[0], store_sem.at[1])
    for load in loads:
        load.start()
    stays.start()
    loads[0].wait()
    moving = moves_s[g] != g

    @pl.when(moving)
    def _():
        renews.start()

    @pl.when(jnp.logical_not(moving))
    def _():
        keeps.start()

    loads[1].wait()
    loads[2].wait()
    for jj in range(own):
        for q in range(group):
            lanes = pl.ds((jj * group + q) * LANES, LANES)
            late = group + q
            moved = jnp.where(moving, moved_v[jj, q : q + 1], heads_v[jj, 0, late : late + 1])
            first_v[:, lanes] = jnp.concatenate(
                [heads_v[jj, r, q : q + 1] for r in range(rows)], axis=0
            ).astype(BF16)
            second_v[:, lanes] = jnp.concatenate(
                [moved, heads_v[jj, 1, late : late + 1]], axis=0
            ).astype(BF16)
    out = [
        pltpu.make_async_copy(first_v, first_out, store_sem.at[2]),
        pltpu.make_async_copy(second_v, second_out, store_sem.at[3]),
    ]
    for copy in out:
        copy.start()
    stays.wait()
    keeps.wait()
    for copy in out:
        copy.wait()


def settle(moves, got, stage, heads_out, moved_out):
    own, rows, both, _ = heads_out.shape
    out = jax.ShapeDtypeStruct((rows, own * moved_out.shape[1] * LANES), BF16)
    anywhere = pl.BlockSpec(memory_space=pl.ANY)
    return pl.pallas_call(
        settle_kernel,
        out_shape=(jax.ShapeDtypeStruct(stage.shape, stage.dtype), out, out),
        in_specs=[anywhere] * 5,
        out_specs=(anywhere,) * 3,
        scratch_shapes=[
            pltpu.SMEM(moves.shape, jnp.int32),
            pltpu.VMEM(heads_out.shape, F32),
            pltpu.VMEM(moved_out.shape, F32),
            pltpu.VMEM(out.shape, BF16),
            pltpu.VMEM(out.shape, BF16),
            pltpu.SemaphoreType.DMA((3,)),
            pltpu.SemaphoreType.DMA((4,)),
        ],
        compiler_params=pltpu.CompilerParams(vmem_limit_bytes=32 << 20),
        name="settle",
    )(moves, got, stage, heads_out, moved_out)


def on_device(queries, new_keys, new_values, cache, page_table, kept, moves):
    count = lax.axis_size("req")
    bits = count.bit_length() - 1
    branches = [functools.partial(fused, d, bits) for d in range(1, count)]
    pieces = lax.switch(
        moves[0] - 1, branches, cache, queries, new_keys, new_values, page_table, kept
    )
    after, first, second = settle(moves, *pieces)
    return first, second, after


def solution(mesh):
    in_specs = (
        P(None, "req", None),
        P(None, "req", None),
        P(None, "req", None),
        P("req", "blk", None, None),
        P("req", None),
        P(None, "req", None, None),
        P(),
    )
    out_specs = (P("req", "blk"), P("req", "blk"), P("req", "blk", None, None))
    return jax.shard_map(
        on_device, mesh=mesh, in_specs=in_specs, out_specs=out_specs, check_vma=False
    )
```
